128 devices in a mesh: group: 8 (over y, core), shard: 16 (over x, z).
Axes of the slice: x: 4, y: 4, z: 4, core: 2. Of those that a mesh axis runs over, the one named last changes fastest.
Arguments:
- tokens: bfloat16 [1024, 6144], P('group'), may hold values from -6 to 6
- experts: int32 [1024, 2], P('group'), may hold values from 0 to 7, all different within a row; in each aligned block of 128 rows (0 to 127, 128 to 255, ...) at most 64 rows name the same one
- mix_weight: float32 [1024, 2], P('group'), may hold values from 0.2 to 1
- w_gate: bfloat16 [8, 6144, 8192], P('group', None, 'shard'), may hold values from -0.078125 to 0.078125
- w_up: bfloat16 [8, 6144, 8192], P('group', None, 'shard'), may hold values from -0.078125 to 0.078125
- w_down: bfloat16 [8, 8192, 6144], P('group', 'shard'), may hold values from -0.09375 to 0.09375
Outputs:
- mixed: bfloat16 [1024, 6144], P('group', 'shard')
The draws below stay inside these ranges and needn't reach their ends.
Inputs may be any that keep to these rules, and one draw needn't show every extreme that they name: Each token names 2 different experts. Among the tokens of one group no expert is named more than 64 times, a bound that some block reaches.
All inputs are finite; a program needn't handle non-finite values.
Results may differ from the reference program's by a relative error of at most 0.02.
Values may be sent and summed in bfloat16 or wider, within the bound.
A program may use at most 128 MiB of HBM per device.

```python
import math
import jax
import jax.numpy as jnp
import numpy as np
from jax import lax

D = 6144
FF = 8192
TOPK = 2
TG = 128
CAP = 64
EXPERTS = 8
TOKENS = 1024
N_GROUP = 8
N_SHARD = 16


def spiked(values, stream_key, source, target, parts, factor):
    def block_of(position):
        return (jnp.arange(values.shape[position]) // (values.shape[position] // parts)).reshape((-1,) + (1,) * (values.ndim - 1 - position))

    near = jax.random.permutation(stream_key, parts)[block_of(target)]
    far = (block_of(target) + parts // 2) % parts
    return jnp.where((block_of(source) == near) | (block_of(source) == far), factor * values, values)


def levels(own_key, shape, split, least, top_value):
    loudness = 1.0
    for position, parts in split:
        draws = jax.random.uniform(jax.random.fold_in(jax.random.fold_in(own_key, 6), position), (parts,), jnp.float32, least / len(split), top_value / len(split))
        loudness = loudness * jnp.repeat(jnp.exp(draws), shape[position] // parts).reshape((-1,) + (1,) * (len(shape) - 1 - position))
    return loudness


def shared_out(own_key, own, number, rows, count, top, limit, lean):
    order = jax.random.permutation(own_key, count)
    crowded, ordinary = shares(count, rows * top, limit, lean, True), shares(count, rows * top, limit, lean, False)
    places = jnp.arange(count)

    def named(lengths, turn):
        used = int((lengths > 0).sum())
        fixed = max(1, used // 4)
        passed = fixed + (places - fixed + turn * (used - fixed)) % max(1, count - fixed)
        return jnp.zeros((count,), jnp.int32).at[order[jnp.where(places < fixed, places, passed)]].set(jnp.asarray(lengths, jnp.int32))

    lengths = jnp.where(number % 4 == 0, named(crowded, number // 4), named(ordinary, number - number // 4 - 1))
    mixed = jax.random.permutation(jax.random.fold_in(own, 3), count)
    giver, sink = mixed[0:count // 2 * 2:2], mixed[1:count // 2 * 2:2]
    slack = jnp.minimum(lengths[giver] - 1, limit - lengths[sink]) // 2
    slack = jnp.where((giver == order[0]) | (sink == order[0]) | (lengths[sink] == 0), 0, jnp.maximum(slack, 0))
    passed = jax.random.randint(jax.random.fold_in(own, 4), (count // 2,), 0, 1 << 20) % (slack + 1)
    lengths = lengths.at[giver].add(-passed).at[sink].add(passed)
    items = jnp.searchsorted(jnp.cumsum(lengths), jnp.arange(rows * top), side="right").astype(jnp.int32)
    grid = items.reshape(top, rows).T
    grid = grid[jax.random.permutation(jax.random.fold_in(own, 1), rows)]
    turn = jax.random.randint(jax.random.fold_in(own, 2), (rows, 1), 0, top)
    return jnp.take_along_axis(grid, (jnp.arange(top)[None, :] + turn) % top, axis=1)


def shares(amount, total, limit, lean, full):
    weights = [(1 << 20) // math.isqrt(grade ** lean) + 1 for grade in range(1, amount + 1)]
    largest = limit if full else min(limit, max(-(-total // amount), total * weights[0] // sum(weights)))
    least = 1 if total - largest >= amount - 1 else 0
    given, surplus = [largest] + [least] * (amount - 1), total - largest - least * (amount - 1)
    while surplus > 0:
        movable = [i for i in range(1, amount) if given[i] < largest] or [i for i in range(1, amount) if given[i] < limit]
        pool, remaining = sum([weights[i] for i in movable]), surplus
        for i in movable:
            more = min(limit - given[i], max(1, remaining * weights[i] // pool), surplus)
            given[i] = given[i] + more
            surplus = surplus - more
    return np.array(given)


def bell_draw(key, extent, spread, bound, shards=(), kind=jnp.bfloat16):
    entries = spread * jax.random.normal(key, extent, jnp.float32)
    if shards:
        entries = entries * levels(key, extent, shards, -0.22, 0.18)
    return jnp.clip(entries, -bound, bound).astype(kind)


def noise_with(own_key, shape, spread, most, pieces, heavy, kind=jnp.bfloat16):
    values = spread * jax.random.normal(own_key, shape, jnp.float32)
    if pieces:
        values = values * levels(own_key, shape, pieces, -0.22, 0.18)
    return jnp.clip(spiked(values, jax.random.fold_in(own_key, 3), *heavy), -most, most).astype(kind)


def setup_inputs(seed: int = 0) -> dict:
    streams_of = jax.random.split(jax.random.key(seed), 7)
    tokens = bell_draw(streams_of[0], (TOKENS, D), 1.0, 6.0, ((0, 8),))
    experts_keys = jax.random.split(jax.random.fold_in(streams_of[1], 1), TOKENS // TG)
    experts_turns = jax.random.permutation(jax.random.fold_in(streams_of[1], 3), TOKENS // TG)
    experts = jax.vmap(lambda own, number: shared_out(jax.random.fold_in(streams_of[1], 2), own, number, TG, EXPERTS, TOPK, CAP, 2))(experts_keys, experts_turns).reshape((TOKENS, TOPK))
    mix_weight = jnp.clip(0.2 + 0.8 * jax.random.uniform(streams_of[2], (TOKENS, TOPK), jnp.float32) ** levels(streams_of[2], (TOKENS, TOPK), ((0, 8),), -0.2, 0.2), 0.2, 1.0)
    w_gate = bell_draw(streams_of[3], (EXPERTS, D, FF), D ** -0.5, 0.078125, ((0, 8), (2, 16)))
    w_up = bell_draw(streams_of[4], (EXPERTS, D, FF), D ** -0.5, 0.078125, ((0, 8), (2, 16)))
    w_down = noise_with(streams_of[5], (EXPERTS, FF, D), FF ** -0.5, 0.09375, ((0, 8), (1, 16)), (1, 2, 16, 2.0))
    return dict(tokens=tokens, experts=experts, mix_weight=mix_weight, w_gate=w_gate, w_up=w_up, w_down=w_down)


def slot_plan(chosen, experts_total, capacity, reach):
    count = chosen.shape[0]
    labels = jnp.arange(experts_total, dtype=jnp.int32)
    onehot = (chosen[:, None] == labels[None, :]).astype(jnp.int32)
    before = jnp.cumsum(onehot, axis=0) - onehot
    slot_rank = jnp.sum(before * onehot, axis=1).astype(jnp.int32)
    route_ids = jnp.arange(count, dtype=jnp.int32)
    slots = jnp.arange(capacity, dtype=jnp.int32)
    matches = (chosen[None, None, :] == labels[:, None, None]) & (slot_rank[None, None, :] == slots[None, :, None])
    filled = jnp.any(matches, axis=2)
    source_row = jnp.sum(jnp.where(matches, route_ids[None, None, :] // reach, 0), axis=2).astype(jnp.int32)
    return slot_rank, source_row, filled


def expert_output(arrived, gate_w, up_w, down_w):
    piece = FF // N_SHARD
    rows = arrived.astype(jnp.float32)
    total = jnp.zeros((arrived.shape[0], D), jnp.float32)
    for shard_id in range(N_SHARD):
        lower = shard_id * piece
        gate = jnp.dot(rows, gate_w[:, lower:lower + piece].astype(jnp.float32), precision=lax.Precision.HIGHEST)
        up = jnp.dot(rows, up_w[:, lower:lower + piece].astype(jnp.float32), precision=lax.Precision.HIGHEST)
        hidden = (jax.nn.silu(gate) * up).astype(jnp.bfloat16)
        partial_value = jnp.dot(hidden.astype(jnp.float32), down_w[lower:lower + piece, :].astype(jnp.float32), precision=lax.Precision.HIGHEST).astype(jnp.bfloat16)
        total = total + partial_value.astype(jnp.float32)
    return total.astype(jnp.bfloat16)


def reference(tokens, experts, mix_weight, w_gate, w_up, w_down):
    tok_groups = tokens.reshape(N_GROUP, TG, D)
    chosen = experts.reshape(N_GROUP, TG * TOPK)
    slot_rank, source_row, filled = jax.vmap(lambda c: slot_plan(c, EXPERTS, CAP, TOPK))(chosen)

    def pick_rows(group_tokens, rows, used):
        return jnp.where(used[:, :, None], group_tokens[rows], jnp.zeros((), group_tokens.dtype))

    outgoing = jax.vmap(pick_rows)(tok_groups, source_row, filled)
    per_expert = jnp.transpose(outgoing, (1, 0, 2, 3)).reshape(EXPERTS, N_GROUP * CAP, D)
    results = lax.map(lambda item: expert_output(*item), (per_expert, w_gate, w_up, w_down))
    home = jnp.transpose(results.reshape(EXPERTS, N_GROUP, CAP, D), (1, 0, 2, 3))
    picked = jax.vmap(lambda h, c, r: h[c, r])(home, chosen, slot_rank)
    picked = picked.reshape(TOKENS, TOPK, D).astype(jnp.float32)
    mixed = jnp.sum(mix_weight[:, :, None] * picked, axis=1)
    return mixed.astype(jnp.bfloat16)
```

```python
import functools

import jax
import jax.numpy as jnp
from jax import lax
from jax.experimental import pallas as pl
from jax.experimental.pallas import tpu as pltpu
from jax.sharding import PartitionSpec as P

MESH = pl.DeviceIdType.MESH
F32, BF16 = jnp.float32, jnp.bfloat16
NX = 4
TG = 128
CAP = 64
KB = 768
FFS = 512
HALF = 3072
CHUNKS = 2
ROWS = TG // CHUNKS
COLS = 512


def kernel(
    tok, ex, mw, wg_hbm, wu_hbm, wd_hbm, out,
    wg, wu, wd, land, meta, pick, back, wslot, xown, xsend, xsib, acc_g, acc_u, hid,
    pcat, psend, t0, t1, t2, rb1, rb2, rb3,
    local_sem, send_sem, recv_sem,
):
    group, shard = lax.axis_index("group"), lax.axis_index("shard")
    x, y, z, c = shard // NX, group // 2, shard % NX, group % 2
    sib = 1 - c

    def dev(x, y, z, c):
        return ((y % NX) * 2 + c, (x % NX) * NX + z % NX)

    def on_ring(d):
        return dev(x + d * (1 - c) + NX, y, z + d * c + NX, c)

    def ring_place(core):
        return x * (1 - core) + z * core

    r = ring_place(c)

    used = [0]

    def remote(src, dst, device):
        i = used[0]
        used[0] += 1
        return pltpu.make_async_remote_copy(
            src_ref=src, dst_ref=dst, send_sem=send_sem.at[i], recv_sem=recv_sem.at[i],
            device_id=device, device_id_type=MESH,
        )

    sent = []

    def go(copy):
        copy.start()
        sent.append(copy)
        return copy

    peers = [((y + dy) % NX, c if dc == 0 else sib) for dy in range(NX) for dc in range(2) if dy or dc]
    partners = [dev(x, py, z, pc) for py, pc in peers]
    partners += [dev(x + 1, y, z, c), dev(x + NX - 1, y, z, c), dev(x, y, z + 1, c), dev(x, y, z + NX - 1, c)]
    barrier = pltpu.get_barrier_semaphore()
    for partner in partners:
        pl.semaphore_signal(barrier, inc=1, device_id=partner, device_id_type=MESH)

    load_g = pltpu.make_async_copy(wg_hbm.at[0], wg, local_sem.at[0])
    load_u = pltpu.make_async_copy(wu_hbm.at[0], wu, local_sem.at[1])
    own_loads = [
        pltpu.make_async_copy(
            tok.at[:, pl.ds(pl.multiple_of(c * HALF + q * KB, KB), KB)], land.at[q, y, c], local_sem.at[3 + q]
        )
        for q in range(NX)
    ]
    for copy in own_loads:
        copy.start()

    meta[group] = jnp.zeros((8, TG), F32)
    meta[group, 0:2] = ex[...].astype(F32)
    meta[group, 2:4] = mw[...]

    pl.semaphore_wait(barrier, len(partners))

    plans = [go(remote(meta.at[group], meta.at[group], dev(x, py, z, pc))) for py, pc in peers]

    def token_block(core, q, h):
        return tok.at[pl.ds(h * ROWS, ROWS), pl.ds(pl.multiple_of(core * HALF + q * KB, KB), KB)]

    direct = {}
    for h in range(CHUNKS):
        for step in (1, -1):
            for dc in range(2):
                core = c if dc == 0 else sib
                q = ring_place(core)
                direct[h, step, dc] = go(
                    remote(
                        token_block(core, q, h),
                        land.at[q, y, c, pl.ds(h * ROWS, ROWS)],
                        dev(x, y + step + NX, z, core),
                    )
                )
    load_g.start()
    load_u.start()
    across = [
        go(
            remote(
                tok.at[:, pl.ds(pl.multiple_of(sib * HALF + q * KB, KB), KB)], land.at[q, y, c], dev(x, y, z, sib)
            )
        )
        for q in range(NX)
    ]

    def load_down(i, carry):
        j, b = i // 16, i % 16
        place = jnp.where(j == 2, (b % NX) * NX + b // NX, b)
        pltpu.make_async_copy(
            wd_hbm.at[0, :, pl.ds(pl.multiple_of(b * 384 + j * 128, 128), 128)],
            wd.at[j, :, pl.ds(pl.multiple_of(place * 128, 128), 128)],
            local_sem.at[2],
        ).start()
        return carry

    lax.fori_loop(0, 48, load_down, 0)

    for copy in plans:
        copy.wait_recv()
    own_e = group.astype(F32)
    sib_e = (2 * y + sib).astype(F32)
    before = lax.broadcasted_iota(jnp.int32, (TG, TG), 0) < lax.broadcasted_iota(jnp.int32, (TG, TG), 1)
    before = jnp.where(before, 1.0, 0.0).astype(BF16)
    slot = lax.broadcasted_iota(jnp.int32, (CAP, TG), 0).astype(F32)
    first, second = meta[:, 0, :], meta[:, 1, :]
    first_w, second_w = meta[:, 2, :], meta[:, 3, :]
    plan = []
    for e in (own_e, sib_e):
        named = jnp.where((first == e) | (second == e), 1.0, 0.0)
        rank = jnp.dot(named.astype(BF16), before, preferred_element_type=F32)
        plan.append(jnp.where(named > 0.5, rank, -1.0))
    weight = jnp.where(first == own_e, first_w, 0.0) + jnp.where(second == own_e, second_w, 0.0)
    for g in range(8):
        py, pc = g // 2, g % 2
        rows = [jnp.where(p[g : g + 1, :] == slot, 1.0, 0.0) for p in plan]
        onehot = jnp.concatenate(rows, axis=0)
        pick[g] = onehot.astype(BF16)
        back[pc, py] = onehot.T.astype(BF16)
        total = jnp.sum(rows[0] * weight[g : g + 1, :], axis=1, keepdims=True)
        wslot[pl.ds((pc * 4 + py) * CAP, CAP)] = jnp.broadcast_to(total, (CAP, 128))

    ring_own, relay_y, ring_relay = {}, {}, {}

    def forward(h, dy):
        block = land.at[r, (y + dy) % NX, :, pl.ds(h * ROWS, ROWS)]
        for d in (1, -1):
            ring_own[h, dy, d] = go(remote(block, block, on_ring(d)))

    for h in range(CHUNKS):
        for dy, step in ((3, 1), (1, -1)):
            for dc in range(2):
                direct[h, step, dc].wait_recv()
            block = land.at[r, (y + dy) % NX, 1 if step == 1 else 0, pl.ds(h * ROWS, ROWS)]
            relay_y[h, step] = go(remote(block, block, dev(x, y + step + NX, z, c)))
            forward(h, dy)

    def pass_on(h, dy):
        for d in (1, -1):
            ring_own[h, dy, d].wait_recv()
            block = land.at[(r - d + NX) % NX, (y + dy) % NX, 1 if d == 1 else 0, pl.ds(h * ROWS, ROWS)]
            ring_relay[h, dy, d] = go(remote(block, block, on_ring(d)))

    for h in range(CHUNKS):
        for step in (1, -1):
            relay_y[h, step].wait_recv()
        forward(h, 2)
        for dy in (3, 1):
            pass_on(h, dy)
    for copy in own_loads:
        copy.wait()
    for copy in across:
        copy.wait_recv()
    load_g.wait()
    load_u.wait()

    acc_g[...] = jnp.zeros_like(acc_g)
    acc_u[...] = jnp.zeros_like(acc_u)
    cross = []

    def select(i, q):
        def one(g, carry):
            py, pc = g // 2, g % 2
            rows = jnp.dot(pick[g], land[q, py, pc], preferred_element_type=F32).astype(BF16)
            place = pl.ds(pl.multiple_of((pc * 4 + py) * CAP, CAP), CAP)
            xown[place, :] = rows[0:CAP]
            xsend[i, place, :] = rows[CAP:]
            return carry

        lax.fori_loop(0, 8, one, 0)
        cross.append(go(remote(xsend.at[i], xsib.at[i], dev(x, y, z, sib))))

    def gate_up(rows_ref, start):
        depth = pl.ds(pl.multiple_of(start, KB), KB)

        def one(m, carry):
            place = pl.ds(pl.multiple_of(m * 256, 256), 256)
            rows = rows_ref[place, :]
            acc_g[place, :] += jnp.dot(rows, wg[depth, :], preferred_element_type=F32)
            acc_u[place, :] += jnp.dot(rows, wu[depth, :], preferred_element_type=F32)
            return carry

        lax.fori_loop(0, 2, one, 0)

    order = (0, 1, 3, 2)
    places = [(r + d) % NX for d in order]
    sib_places = [(ring_place(sib) + d) % NX for d in order]

    def own_block(i):
        select(i, places[i])
        gate_up(xown, c * HALF + places[i] * KB)

    def sib_block(i):
        cross[i].wait_recv()
        gate_up(xsib.at[i], sib * HALF + sib_places[i] * KB)

    own_block(0)
    for h in range(CHUNKS):
        pass_on(h, 2)
    own_block(1)
    own_block(2)
    sib_block(0)
    sib_block(1)
    for h in range(CHUNKS):
        for dy in (3, 1, 2):
            for d in (1, -1):
                ring_relay[h, dy, d].wait_recv()
    own_block(3)
    sib_block(2)
    sib_block(3)

    def activate(m, carry):
        place = pl.ds(pl.multiple_of(m * 128, 128), 128)
        gate, up = acc_g[place, :], acc_u[place, :]
        hid[place, :] = (jax.nn.silu(gate) * up * wslot[place, 0:1]).astype(BF16)
        return carry

    lax.fori_loop(0, 4, activate, 0)

    pltpu.make_async_copy(wd, wd, local_sem.at[2]).wait()
    ts = (t0, t1, t2)
    at = ((x, y, z), (y, z, x), (z, x, y))
    steps = (
        (lambda d: dev(x + d + NX, y, z, c)),
        (lambda d: dev(x, y + d + NX, z, c)),
        (lambda d: dev(x, y, z + d + NX, c)),
    )
    swap = {}

    def down(n, j, a):
        columns = pl.ds(pl.multiple_of(a * COLS, COLS), COLS)
        w = wd[j, :, columns]
        theirs = jnp.dot(hid[pl.ds(pl.multiple_of(sib * 256, 256), 256), :], w, preferred_element_type=F32)
        psend[n] = theirs.astype(BF16).reshape(4, CAP, COLS)
        swap[n] = go(remote(psend.at[n], pcat.at[n, :, pl.ds(CAP, CAP), :], dev(x, y, z, sib)))
        ours = jnp.dot(hid[pl.ds(pl.multiple_of(c * 256, 256), 256), :], w, preferred_element_type=F32)
        pcat[n, :, 0:CAP, :] = ours.astype(BF16).reshape(4, CAP, COLS)

    def combine(n, j, a):
        swap[n].wait_recv()
        for py in range(4):
            rows = jnp.dot(back[c, py], pcat[n, py], preferred_element_type=F32).astype(BF16)
            for b in range(4):
                part = rows[:, b * 128 : (b + 1) * 128]
                if j == 0:
                    t0[a, py, b] = part
                elif j == 1:
                    t1[py, b, a] = part
                else:
                    t2[a, b, py] = part

    copies = {}

    def start(j, level, t, buf, place, axis, kind):
        size = t.shape[1] // 2
        far, right, left = (place + 2) % NX, (place + 1) % NX, (place + 3) % NX
        low, high = pl.ds(0, size), pl.ds(size, size)
        src = {
            "R1a": t.at[far, low], "L1a": t.at[far, high], "R1b": t.at[right, high],
            "L1b": t.at[left, low], "R2": t.at[right, low], "L2": t.at[left, high],
        }[kind]
        slot_of = ("R1a", "L1a", "R1b", "L1b", "R2", "L2").index(kind)
        copies[j, level, kind] = go(remote(src, buf.at[j, slot_of], steps[axis](1 if kind[0] == "R" else -1)))

    def add(t, index, low, size, *bufs):
        place = pl.ds(low, size)
        total = t[index, place].astype(F32)
        for buf in bufs:
            total = total + buf[...].astype(F32)
        t[index, place] = total.astype(BF16)

    def middle(j, level, t, buf, place, axis):
        size = t.shape[1] // 2
        copies[j, level, "R1a"].wait_recv()
        add(t, (place + 1) % NX, 0, size, buf.at[j, 0])
        start(j, level, t, buf, place, axis, "R2")
        copies[j, level, "L1a"].wait_recv()
        add(t, (place + 3) % NX, size, size, buf.at[j, 1])
        start(j, level, t, buf, place, axis, "L2")

    def finish(j, level, t, buf, place, axis):
        size = t.shape[1] // 2
        for kind in ("R1b", "L1b", "R2", "L2"):
            copies[j, level, kind].wait_recv()
        add(t, place, 0, size, buf.at[j, 4], buf.at[j, 3])
        add(t, place, size, size, buf.at[j, 2], buf.at[j, 5])

    axes = ((0, 1, 2), (1, 2, 0), (2, 0, 1))

    def args(j, level):
        t = ts[j]
        for l in range(level):
            t = t.at[at[j][l]]
        return (j, level, t, (rb1, rb2, rb3)[level], at[j][level], axes[j][level])

    chunks = [(1, 0, 0), (1, 0, 1), (1, 0, 2), (1, 0, 3)]
    chunks += [(0, x, 2), (2, z, 2), (0, x, 1), (0, x, 3), (2, z, 1), (2, z, 3), (0, x, 0), (2, z, 0)]

    def after(j, k):
        if j == 1:
            if k == 3:
                for kind in ("R1a", "L1a", "R1b", "L1b"):
                    start(*args(1, 0), kind)
        elif k == 2:
            start(*args(j, 0), "R1a")
            start(*args(j, 0), "L1a")
        elif k == 1:
            start(*args(j, 0), "R1b")
        elif k == 3:
            start(*args(j, 0), "L1b")

    lag = 1
    for n in range(len(chunks) + lag):
        if n < len(chunks):
            j, base, k = chunks[n]
            down(n, j, (base + k) % NX)
        if n >= lag:
            j, base, k = chunks[n - lag]
            combine(n - lag, j, (base + k) % NX)
            after(j, k)

    for level in range(3):
        if level:
            for j in (1, 0, 2):
                for kind in ("R1a", "L1a", "R1b", "L1b"):
                    start(*args(j, level), kind)
        for j in (1, 0, 2):
            middle(*args(j, level))
        for j in (1, 0, 2):
            finish(*args(j, level))
    for j in range(3):
        out[:, j * 128 : (j + 1) * 128] = ts[j][at[j][0], at[j][1], at[j][2]]
    for copy in sent:
        copy.wait_send()


MESSAGES = 7 + 4 * CHUNKS + 4 + 2 * CHUNKS + 6 * CHUNKS + 6 * CHUNKS + 4 + 12 + 54


def local(tokens, experts, mix_weight, w_gate, w_up, w_down):
    any_spec = pl.BlockSpec(memory_space=pl.ANY)
    vmem_spec = pl.BlockSpec(memory_space=pltpu.VMEM)
    return pl.pallas_call(
        kernel,
        out_shape=jax.ShapeDtypeStruct((TG, 384), BF16),
        in_specs=[any_spec, vmem_spec, vmem_spec, any_spec, any_spec, any_spec],
        out_specs=vmem_spec,
        scratch_shapes=[
            pltpu.VMEM((6144, FFS), BF16),
            pltpu.VMEM((6144, FFS), BF16),
            pltpu.VMEM((3, FFS, 2048), BF16),
            pltpu.VMEM((4, 4, 2, TG, KB), BF16),
            pltpu.VMEM((8, 8, TG), F32),
            pltpu.VMEM((8, TG, TG), BF16),
            pltpu.VMEM((2, 4, TG, TG), BF16),
            pltpu.VMEM((512, 128), F32),
            pltpu.VMEM((512, KB), BF16),
            pltpu.VMEM((4, 512, KB), BF16),
            pltpu.VMEM((4, 512, KB), BF16),
            pltpu.VMEM((512, FFS), F32),
            pltpu.VMEM((512, FFS), F32),
            pltpu.VMEM((512, FFS), BF16),
            pltpu.VMEM((12, 4, 2 * CAP, COLS), BF16),
            pltpu.VMEM((12, 4, CAP, COLS), BF16),
            pltpu.VMEM((4, 4, 4, 128, 128), BF16),
            pltpu.VMEM((4, 4, 4, 128, 128), BF16),
            pltpu.VMEM((4, 4, 4, 128, 128), BF16),
            pltpu.VMEM((3, 6, 2, 4, 128, 128), BF16),
            pltpu.VMEM((3, 6, 2, 128, 128), BF16),
            pltpu.VMEM((3, 6, 64, 128), BF16),
            pltpu.SemaphoreType.DMA((7,)),
            pltpu.SemaphoreType.DMA((MESSAGES,)),
            pltpu.SemaphoreType.DMA((MESSAGES,)),
        ],
        compiler_params=pltpu.CompilerParams(
            collective_id=0, has_side_effects=True, vmem_limit_bytes=62 * 2**20
        ),
        name="expert_layer",
    )(tokens, experts.T, mix_weight.T, w_gate, w_up, w_down)


def solution(mesh):
    placed = (
        P("group", None),
        P("group", None),
        P("group", None),
        P("group", None, "shard"),
        P("group", None, "shard"),
        P("group", "shard", None),
    )
    return jax.shard_map(
        local, mesh=mesh, in_specs=placed, out_specs=P("group", "shard"), check_vma=False
    )
```

```python
import functools

import jax
import jax.numpy as jnp
from jax import lax
from jax.experimental import pallas as pl
from jax.experimental.pallas import tpu as pltpu
from jax.sharding import PartitionSpec as P

MESH = pl.DeviceIdType.MESH
F32, BF16 = jnp.float32, jnp.bfloat16
NX = 4
TG = 128
CAP = 64
KB = 768
FFS = 512
HALF = 3072
CHUNKS = 4
LAG = 2
ROWS = TG // CHUNKS
COLS = 512


def kernel(
    tok, ex, mw, wg_hbm, wu_hbm, wd_hbm, out,
    wg, wu, wd, land, meta, pick, back, wslot, xown, xsend, xsib, acc_g, acc_u, hid,
    pcat, psend, t0, t1, t2, rb1, rb2, rb3,
    local_sem, send_sem, recv_sem,
):
    group, shard = lax.axis_index("group"), lax.axis_index("shard")
    x, y, z, c = shard // NX, group // 2, shard % NX, group % 2
    sib = 1 - c

    def dev(x, y, z, c):
        return ((y % NX) * 2 + c, (x % NX) * NX + z % NX)

    def on_ring(d):
        return dev(x + d * (1 - c) + NX, y, z + d * c + NX, c)

    def ring_place(core):
        return x * (1 - core) + z * core

    r = ring_place(c)

    used = [0]

    def remote(src, dst, device):
        i = used[0]
        used[0] += 1
        return pltpu.make_async_remote_copy(
            src_ref=src, dst_ref=dst, send_sem=send_sem.at[i], recv_sem=recv_sem.at[i],
            device_id=device, device_id_type=MESH,
        )

    sent = []

    def go(copy):
        copy.start()
        sent.append(copy)
        return copy

    peers = [((y + dy) % NX, c if dc == 0 else sib) for dy in range(NX) for dc in range(2) if dy or dc]
    partners = [dev(x, py, z, pc) for py, pc in peers]
    partners += [dev(x + 1, y, z, c), dev(x + NX - 1, y, z, c), dev(x, y, z + 1, c), dev(x, y, z + NX - 1, c)]
    barrier = pltpu.get_barrier_semaphore()
    for partner in partners:
        pl.semaphore_signal(barrier, inc=1, device_id=partner, device_id_type=MESH)

    load_g = pltpu.make_async_copy(wg_hbm.at[0], wg, local_sem.at[0])
    load_u = pltpu.make_async_copy(wu_hbm.at[0], wu, local_sem.at[1])
    own_loads = [
        pltpu.make_async_copy(
            tok.at[:, pl.ds(pl.multiple_of(c * HALF + q * KB, KB), KB)], land.at[q, y, c], local_sem.at[3 + q]
        )
        for q in range(NX)
    ]
    for copy in own_loads:
        copy.start()

    meta[group] = jnp.zeros((8, TG), F32)
    meta[group, 0:2] = ex[...].astype(F32)
    meta[group, 2:4] = mw[...]

    pl.semaphore_wait(barrier, len(partners))

    plans = [go(remote(meta.at[group], meta.at[group], dev(x, py, z, pc))) for py, pc in peers]

    def token_block(core, q, h):
        return tok.at[pl.ds(h * ROWS, ROWS), pl.ds(pl.multiple_of(core * HALF + q * KB, KB), KB)]

    direct = {}

    def send_along_y(h, d, copies):
        for step in (1, -1):
            for dc in range(2):
                core = c if dc == 0 else sib
                q = (ring_place(core) + d) % NX
                copies[h, step, dc] = go(
                    remote(
                        token_block(core, q, h),
                        land.at[q, y, c, pl.ds(h * ROWS, ROWS)],
                        dev(x, y + step + NX, z, core),
                    )
                )

    for h in range(CHUNKS):
        send_along_y(h, 0, direct)
    load_g.start()
    load_u.start()
    across = [
        go(
            remote(
                tok.at[:, pl.ds(pl.multiple_of(sib * HALF + q * KB, KB), KB)], land.at[q, y, c], dev(x, y, z, sib)
            )
        )
        for q in range(NX)
    ]

    def load_down(i, carry):
        j, b = i // 16, i % 16
        place = jnp.where(j == 0, b, (b % NX) * NX + b // NX)
        pltpu.make_async_copy(
            wd_hbm.at[0, :, pl.ds(pl.multiple_of(b * 384 + j * 128, 128), 128)],
            wd.at[j, :, pl.ds(pl.multiple_of(place * 128, 128), 128)],
            local_sem.at[2],
        ).start()
        return carry

    lax.fori_loop(0, 48, load_down, 0)

    STEPS = ((0, 2), (1, 3))

    for copy in plans:
        copy.wait_recv()
    own_e = group.astype(F32)
    sib_e = (2 * y + sib).astype(F32)
    before = lax.broadcasted_iota(jnp.int32, (TG, TG), 0) < lax.broadcasted_iota(jnp.int32, (TG, TG), 1)
    before = jnp.where(before, 1.0, 0.0).astype(BF16)
    slot = lax.broadcasted_iota(jnp.int32, (CAP, TG), 0).astype(F32)
    first, second = meta[:, 0, :], meta[:, 1, :]
    first_w, second_w = meta[:, 2, :], meta[:, 3, :]
    plan = []
    for e in (own_e, sib_e):
        named = jnp.where((first == e) | (second == e), 1.0, 0.0)
        rank = jnp.dot(named.astype(BF16), before, preferred_element_type=F32)
        plan.append(jnp.where(named > 0.5, rank, -1.0))
    weight = jnp.where(first == own_e, first_w, 0.0) + jnp.where(second == own_e, second_w, 0.0)
    for py in range(NX):
        for pc in range(2):
            g = 2 * py + pc
            rows = [jnp.where(p[g : g + 1, :] == slot, 1.0, 0.0) for p in plan]
            onehot = jnp.concatenate(rows, axis=0)
            pick[g] = onehot.astype(BF16)
            back[pc, py] = onehot.T.astype(BF16)
            total = jnp.sum(rows[0] * weight[g : g + 1, :], axis=1, keepdims=True)
            wslot[g] = jnp.broadcast_to(total, (CAP, 128))

    ring_own, relay_y, ring_relay, wide = {}, {}, {}, {}

    def forward(h, dy):
        block = land.at[r, (y + dy) % NX, :, pl.ds(h * ROWS, ROWS)]
        for d in (1, -1):
            ring_own[h, dy, d] = go(remote(block, block, on_ring(d)))

    def pass_on(h, dy):
        for d in (1, -1):
            ring_own[h, dy, d].wait_recv()
            if dy == 2:
                block = land.at[(r - d + NX) % NX, (y + dy) % NX, 1 if d == 1 else 0, pl.ds(h * ROWS, ROWS)]
                ring_relay[h, dy, d] = go(remote(block, block, on_ring(d)))

    for h in range(CHUNKS):
        for dy, step in ((3, 1), (1, -1)):
            for dc in range(2):
                direct[h, step, dc].wait_recv()
            block = land.at[r, (y + dy) % NX, 1 if step == 1 else 0, pl.ds(h * ROWS, ROWS)]
            relay_y[h, step] = go(remote(block, block, dev(x, y + step + NX, z, c)))
            forward(h, dy)
    for h in range(CHUNKS):
        send_along_y(h, 2, wide)
    for copy in own_loads:
        copy.wait()
    for copy in across:
        copy.wait_recv()
    load_g.wait()
    load_u.wait()

    cross = {}

    def select(i, q, half):
        for g in range(4):
            k, pc = g % 2, g // 2
            py = (y + 2 * k + half) % NX
            rows = jnp.dot(pick[2 * py + pc], land[q, py, pc], preferred_element_type=F32).astype(BF16)
            place = pl.ds(half * 256 + g * CAP, CAP)
            xown[place, :] = rows[0:CAP]
            xsend[i, place, :] = rows[CAP:]

        part = pl.ds(half * 256, 256)
        cross[i, half] = go(remote(xsend.at[i, part], xsib.at[i, part], dev(x, y, z, sib)))

    def gate_up(rows_ref, start, half, fresh):
        depth = pl.ds(pl.multiple_of(start, KB), KB)
        place = pl.ds(half * 256, 256)
        rows = rows_ref[place, :]
        for acc, w in ((acc_g, wg), (acc_u, wu)):
            part = jnp.dot(rows, w[depth, :], preferred_element_type=F32)
            if fresh:
                acc[place, :] = part
            else:
                acc[place, :] += part

    order = (0, 1, 3, 2)
    places = [(r + d) % NX for d in order]
    sib_places = [(ring_place(sib) + d) % NX for d in order]

    def own_block(i, half):
        select(i, places[i], half)
        gate_up(xown, c * HALF + places[i] * KB, half, i == 0)

    def sib_block(i, half):
        cross[i, half].wait_recv()
        gate_up(xsib.at[i], sib * HALF + sib_places[i] * KB, half, False)

    def activate(half):
        for g in range(4):
            k, pc = g % 2, g // 2
            place = pl.ds(half * 256 + g * CAP, CAP)
            gate, up = acc_g[place, :], acc_u[place, :]
            scale = wslot[2 * ((y + 2 * k + half) % NX) + pc][:, 0:1]
            hid[place, :] = (jax.nn.silu(gate) * up * scale).astype(BF16)

    own_block(0, 1)
    for h in range(CHUNKS):
        for step in (1, -1):
            relay_y[h, step].wait_recv()
        forward(h, 2)
    own_block(0, 0)
    for h in range(CHUNKS):
        for dy in (3, 1):
            pass_on(h, dy)
    sib_block(0, 1)
    own_block(1, 1)
    for h in range(CHUNKS):
        pass_on(h, 2)
    own_block(2, 1)
    own_block(1, 0)
    own_block(2, 0)
    sib_block(0, 0)
    sib_block(1, 1)
    sib_block(2, 1)
    for copy in ring_relay.values():
        copy.wait_recv()
    own_block(3, 0)
    sib_block(1, 0)
    sib_block(2, 0)
    for copy in wide.values():
        copy.wait_recv()
    own_block(3, 1)
    sib_block(3, 0)
    activate(0)
    sib_block(3, 1)
    activate(1)

    pltpu.make_async_copy(wd, wd, local_sem.at[2]).wait()
    ts = (t0, t1, t2)
    at = ((x, y, z), (y, z, x), (z, x, y))
    steps = (
        (lambda d: dev(x + d + NX, y, z, c)),
        (lambda d: dev(x, y + d + NX, z, c)),
        (lambda d: dev(x, y, z + d + NX, c)),
    )
    swap = {}

    def down(n, j, a):
        columns = pl.ds(pl.multiple_of(a * COLS, COLS), COLS)
        w = wd[j, :, columns]
        def rows_of(core):
            first, second = (pl.ds(pl.multiple_of(half * 256 + core * 128, 128), 128) for half in range(2))
            rows = jnp.concatenate([hid[first, :], hid[second, :]], axis=0)
            return jnp.dot(rows, w, preferred_element_type=F32).astype(BF16).reshape(4, CAP, COLS)

        psend[n] = rows_of(sib)
        swap[n] = go(remote(psend.at[n], pcat.at[n, :, pl.ds(CAP, CAP), :], dev(x, y, z, sib)))
        pcat[n, :, 0:CAP, :] = rows_of(c)

    def combine(n, j, a):
        swap[n].wait_recv()
        for i in range(4):
            py = (y + STEPS[i // 2][i % 2]) % NX
            rows = jnp.dot(back[c, py], pcat[n, i], preferred_element_type=F32).astype(BF16)
            for b in range(4):
                part = rows[:, b * 128 : (b + 1) * 128]
                if j == 0:
                    t0[a, py, b] = part
                elif j == 1:
                    t1[py, a, b] = part
                else:
                    t2[a, b, py] = part

    copies = {}

    def start(j, level, t, buf, place, axis, kind):
        size = t.shape[1] // 2
        far, right, left = (place + 2) % NX, (place + 1) % NX, (place + 3) % NX
        low, high = pl.ds(0, size), pl.ds(size, size)
        src = {
            "R1a": t.at[far, low], "L1a": t.at[far, high], "R1b": t.at[right, high],
            "L1b": t.at[left, low], "R2": t.at[right, low], "L2": t.at[left, high],
        }[kind]
        slot_of = ("R1a", "L1a", "R1b", "L1b", "R2", "L2").index(kind)
        copies[j, level, kind] = go(remote(src, buf.at[j, slot_of], steps[axis](1 if kind[0] == "R" else -1)))

    def add(t, index, low, size, *bufs):
        place = pl.ds(low, size)
        total = t[index, place].astype(F32)
        for buf in bufs:
            total = total + buf[...].astype(F32)
        t[index, place] = total.astype(BF16)

    def middle(j, level, t, buf, place, axis):
        size = t.shape[1] // 2
        copies[j, level, "R1a"].wait_recv()
        add(t, (place + 1) % NX, 0, size, buf.at[j, 0])
        start(j, level, t, buf, place, axis, "R2")
        copies[j, level, "L1a"].wait_recv()
        add(t, (place + 3) % NX, size, size, buf.at[j, 1])
        start(j, level, t, buf, place, axis, "L2")

    axes = ((0, 1, 2), (1, 2, 0), (2, 0, 1))

    def args(j, level):
        t = ts[j]
        for l in range(level):
            t = t.at[at[j][l]]
        return (j, level, t, (rb1, rb2, rb3)[level], at[j][level], axes[j][level])

    chunks = [(1, 0, 0), (1, 0, 1), (0, x, 2), (2, z, 2), (1, 0, 2), (1, 0, 3)]
    chunks += [(0, x, 1), (0, x, 3), (2, z, 1), (2, z, 3), (0, x, 0), (2, z, 0)]

    def after(j, k):
        if j == 1:
            for kind in {1: ("R1a", "L1b"), 3: ("L1a", "R1b")}.get(k, ()):
                start(*args(1, 0), kind)
        elif k == 2:
            start(*args(j, 0), "R1a")
            start(*args(j, 0), "L1a")
        elif k == 1:
            start(*args(j, 0), "R1b")
        elif k == 3:
            start(*args(j, 0), "L1b")

    for n in range(len(chunks) + LAG):
        if n < len(chunks):
            j, base, k = chunks[n]
            down(n, j, (base + k) % NX)
        if n >= LAG:
            j, base, k = chunks[n - LAG]
            combine(n - LAG, j, (base + k) % NX)
            after(j, k)

    straight = {}

    def spread(j, level, d):
        _, _, t, buf, place, axis = args(j, level)
        straight[j, level, d] = go(remote(t.at[(place + d) % NX], buf.at[j, d - 1], steps[axis](d)))

    def gather(j, level):
        _, _, t, buf, place, _ = args(j, level)
        total = t[place].astype(F32)
        for d in (1, 2, 3):
            straight[j, level, d].wait_recv()
            total = total + buf[j, d - 1].astype(F32)
        return total

    def finish(j):
        for kind in ("R1b", "L1b", "R2", "L2"):
            copies[j, 0, kind].wait_recv()
        here, second = ts[j].at[at[j][0]], at[j][1]
        for d in (2, 1, 3, 0):
            b = (second + d) % NX
            one, two = jnp.where(b < 2, 4, 2), jnp.where(b < 2, 3, 5)
            total = here[b].astype(F32) + rb1[j, one, b % 2].astype(F32) + rb1[j, two, b % 2].astype(F32)
            here[b] = total.astype(BF16)
            if d:
                spread(j, 1, d)

    for j in (1, 0, 2):
        middle(*args(j, 0))
    for j in (1, 0, 2):
        finish(j)
    for j in (1, 0, 2):
        ts[j][at[j][0], at[j][1]] = gather(j, 1).astype(BF16)
        for d in (2, 1, 3):
            spread(j, 2, d)
    for j in (1, 0, 2):
        out[:, j * 128 : (j + 1) * 128] = gather(j, 2).astype(BF16)
    for copy in sent:
        copy.wait_send()


MESSAGES = 7 + 4 * CHUNKS + 4 + 2 * CHUNKS + 6 * CHUNKS + 6 * CHUNKS + 8 + 12 + 36


def local(tokens, experts, mix_weight, w_gate, w_up, w_down):
    any_spec = pl.BlockSpec(memory_space=pl.ANY)
    vmem_spec = pl.BlockSpec(memory_space=pltpu.VMEM)
    return pl.pallas_call(
        kernel,
        out_shape=jax.ShapeDtypeStruct((TG, 384), BF16),
        in_specs=[any_spec, vmem_spec, vmem_spec, any_spec, any_spec, any_spec],
        out_specs=vmem_spec,
        scratch_shapes=[
            pltpu.VMEM((6144, FFS), BF16),
            pltpu.VMEM((6144, FFS), BF16),
            pltpu.VMEM((3, FFS, 2048), BF16),
            pltpu.VMEM((4, 4, 2, TG, KB), BF16),
            pltpu.VMEM((8, 8, TG), F32),
            pltpu.VMEM((8, TG, TG), BF16),
            pltpu.VMEM((2, 4, TG, TG), BF16),
            pltpu.VMEM((8, CAP, 128), F32),
            pltpu.VMEM((512, KB), BF16),
            pltpu.VMEM((4, 512, KB), BF16),
            pltpu.VMEM((4, 512, KB), BF16),
            pltpu.VMEM((512, FFS), F32),
            pltpu.VMEM((512, FFS), F32),
            pltpu.VMEM((512, FFS), BF16),
            pltpu.VMEM((12, 4, 2 * CAP, COLS), BF16),
            pltpu.VMEM((12, 4, CAP, COLS), BF16),
            pltpu.VMEM((4, 4, 4, 128, 128), BF16),
            pltpu.VMEM((4, 4, 4, 128, 128), BF16),
            pltpu.VMEM((4, 4, 4, 128, 128), BF16),
            pltpu.VMEM((3, 6, 2, 4, 128, 128), BF16),
            pltpu.VMEM((3, 3, 4, 128, 128), BF16),
            pltpu.VMEM((3, 3, 128, 128), BF16),
            pltpu.SemaphoreType.DMA((7,)),
            pltpu.SemaphoreType.DMA((MESSAGES,)),
            pltpu.SemaphoreType.DMA((MESSAGES,)),
        ],
        compiler_params=pltpu.CompilerParams(
            collective_id=0, has_side_effects=True, vmem_limit_bytes=62 * 2**20
        ),
        name="expert_layer",
    )(tokens, experts.T, mix_weight.T, w_gate, w_up, w_down)


def solution(mesh):
    placed = (
        P("group", None),
        P("group", None),
        P("group", None),
        P("group", None, "shard"),
        P("group", None, "shard"),
        P("group", "shard", None),
    )
    return jax.shard_map(
        local, mesh=mesh, in_specs=placed, out_specs=P("group", "shard"), check_vma=False
    )
```

```python
import functools

import jax
import jax.numpy as jnp
from jax import lax
from jax.experimental import pallas as pl
from jax.experimental.pallas import tpu as pltpu
from jax.sharding import PartitionSpec as P

MESH = pl.DeviceIdType.MESH
F32, BF16 = jnp.float32, jnp.bfloat16
NX = 4
TG = 128
CAP = 64
KB = 768
FFS = 512
HALF = 3072
CHUNKS = 4
LAG = 2
ROWS = TG // CHUNKS
COLS = 512


def kernel(
    tok, ex, mw, wg_hbm, wu_hbm, wd_hbm, out,
    wg, wu, wd, land, meta, pick, back, wslot, xown, xsend, xsib, acc_g, acc_u, hid,
    pcat, psend, t0, t1, t2, rb1, rb2, rb3,
    local_sem, send_sem, recv_sem,
):
    group, shard = lax.axis_index("group"), lax.axis_index("shard")
    x, y, z, c = shard // NX, group // 2, shard % NX, group % 2
    sib = 1 - c

    def dev(x, y, z, c):
        return ((y % NX) * 2 + c, (x % NX) * NX + z % NX)

    def on_ring(d):
        return dev(x + d * (1 - c) + NX, y, z + d * c + NX, c)

    def ring_place(core):
        return x * (1 - core) + z * core

    r = ring_place(c)

    used = [0]

    def remote(src, dst, device):
        i = used[0]
        used[0] += 1
        return pltpu.make_async_remote_copy(
            src_ref=src, dst_ref=dst, send_sem=send_sem.at[i], recv_sem=recv_sem.at[i],
            device_id=device, device_id_type=MESH,
        )

    sent = []

    def go(copy):
        copy.start()
        sent.append(copy)
        return copy

    peers = [((y + dy) % NX, c if dc == 0 else sib) for dy in range(NX) for dc in range(2) if dy or dc]
    partners = [dev(x, py, z, pc) for py, pc in peers]
    partners += [dev(x + 1, y, z, c), dev(x + NX - 1, y, z, c), dev(x, y, z + 1, c), dev(x, y, z + NX - 1, c)]
    barrier = pltpu.get_barrier_semaphore()
    for partner in partners:
        pl.semaphore_signal(barrier, inc=1, device_id=partner, device_id_type=MESH)

    load_g = pltpu.make_async_copy(wg_hbm.at[0], wg, local_sem.at[0])
    load_u = pltpu.make_async_copy(wu_hbm.at[0], wu, local_sem.at[1])
    own_loads = [
        pltpu.make_async_copy(
            tok.at[:, pl.ds(pl.multiple_of(c * HALF + q * KB, KB), KB)], land.at[q, y, c], local_sem.at[3 + q]
        )
        for q in range(NX)
    ]
    for copy in own_loads:
        copy.start()

    meta[group] = jnp.zeros((8, TG), F32)
    meta[group, 0:2] = ex[...].astype(F32)
    meta[group, 2:4] = mw[...]

    pl.semaphore_wait(barrier, len(partners))

    plans = [go(remote(meta.at[group], meta.at[group], dev(x, py, z, pc))) for py, pc in peers]

    def token_block(core, q, h):
        return tok.at[pl.ds(h * ROWS, ROWS), pl.ds(pl.multiple_of(core * HALF + q * KB, KB), KB)]

    direct = {}

    def send_along_y(h, d, copies):
        for step in (1, -1):
            for dc in range(2):
                core = c if dc == 0 else sib
                q = (ring_place(core) + d) % NX
                copies[h, step, dc] = go(
                    remote(
                        token_block(core, q, h),
                        land.at[q, y, c, pl.ds(h * ROWS, ROWS)],
                        dev(x, y + step + NX, z, core),
                    )
                )

    for h in range(CHUNKS):
        send_along_y(h, 0, direct)
    load_g.start()
    load_u.start()
    across = [
        go(
            remote(
                tok.at[:, pl.ds(pl.multiple_of(sib * HALF + q * KB, KB), KB)], land.at[q, y, c], dev(x, y, z, sib)
            )
        )
        for q in range(NX)
    ]

    def load_down(i, carry):
        j, b = i // 16, i % 16
        place = jnp.where(j == 0, b, (b % NX) * NX + b // NX)
        pltpu.make_async_copy(
            wd_hbm.at[0, :, pl.ds(pl.multiple_of(b * 384 + j * 128, 128), 128)],
            wd.at[j, :, pl.ds(pl.multiple_of(place * 128, 128), 128)],
            local_sem.at[2],
        ).start()
        return carry

    lax.fori_loop(0, 48, load_down, 0)

    STEPS = ((0, 2), (1, 3))

    for copy in plans:
        copy.wait_recv()
    own_e = group.astype(F32)
    sib_e = (2 * y + sib).astype(F32)
    before = lax.broadcasted_iota(jnp.int32, (TG, TG), 0) < lax.broadcasted_iota(jnp.int32, (TG, TG), 1)
    before = jnp.where(before, 1.0, 0.0).astype(BF16)
    slot = lax.broadcasted_iota(jnp.int32, (CAP, TG), 0).astype(F32)
    first, second = meta[:, 0, :], meta[:, 1, :]
    first_w, second_w = meta[:, 2, :], meta[:, 3, :]
    plan = []
    for e in (own_e, sib_e):
        named = jnp.where((first == e) | (second == e), 1.0, 0.0)
        rank = jnp.dot(named.astype(BF16), before, preferred_element_type=F32)
        plan.append(jnp.where(named > 0.5, rank, -1.0))
    weight = jnp.where(first == own_e, first_w, 0.0) + jnp.where(second == own_e, second_w, 0.0)
    for py in range(NX):
        for pc in range(2):
            g = 2 * py + pc
            rows = [jnp.where(p[g : g + 1, :] == slot, 1.0, 0.0) for p in plan]
            onehot = jnp.concatenate(rows, axis=0)
            pick[g] = onehot.astype(BF16)
            back[pc, py] = onehot.T.astype(BF16)
            total = jnp.sum(rows[0] * weight[g : g + 1, :], axis=1, keepdims=True)
            wslot[g] = jnp.broadcast_to(total, (CAP, 128))

    ring_own, relay_y, ring_relay, wide = {}, {}, {}, {}

    def forward(h, dy):
        block = land.at[r, (y + dy) % NX, :, pl.ds(h * ROWS, ROWS)]
        for d in (1, -1):
            ring_own[h, dy, d] = go(remote(block, block, on_ring(d)))

    def pass_on(h, dy):
        for d in (1, -1):
            ring_own[h, dy, d].wait_recv()
            if dy == 2:
                block = land.at[(r - d + NX) % NX, (y + dy) % NX, 1 if d == 1 else 0, pl.ds(h * ROWS, ROWS)]
                ring_relay[h, dy, d] = go(remote(block, block, on_ring(d)))

    for h in range(CHUNKS):
        for dy, step in ((3, 1), (1, -1)):
            for dc in range(2):
                direct[h, step, dc].wait_recv()
            block = land.at[r, (y + dy) % NX, 1 if step == 1 else 0, pl.ds(h * ROWS, ROWS)]
            relay_y[h, step] = go(remote(block, block, dev(x, y + step + NX, z, c)))
            forward(h, dy)
    for h in range(CHUNKS):
        send_along_y(h, 2, wide)
    for copy in own_loads:
        copy.wait()
    for copy in across:
        copy.wait_recv()
    load_g.wait()
    load_u.wait()

    cross = {}

    def select(i, q, half):
        for g in range(4):
            k, pc = g % 2, g // 2
            py = (y + 2 * k + half) % NX
            rows = jnp.dot(pick[2 * py + pc], land[q, py, pc], preferred_element_type=F32).astype(BF16)
            place = pl.ds(half * 256 + g * CAP, CAP)
            xown[place, :] = rows[0:CAP]
            xsend[i, place, :] = rows[CAP:]

        part = pl.ds(half * 256, 256)
        cross[i, half] = go(remote(xsend.at[i, part], xsib.at[i, part], dev(x, y, z, sib)))

    def gate_up(rows_ref, start, half, fresh):
        depth = pl.ds(pl.multiple_of(start, KB), KB)
        place = pl.ds(half * 256, 256)
        rows = rows_ref[place, :]
        for acc, w in ((acc_g, wg), (acc_u, wu)):
            part = jnp.dot(rows, w[depth, :], preferred_element_type=F32)
            if fresh:
                acc[place, :] = part
            else:
                acc[place, :] += part

    order = (0, 1, 3, 2)
    places = [(r + d) % NX for d in order]
    sib_places = [(ring_place(sib) + d) % NX for d in order]

    def own_block(i, half):
        select(i, places[i], half)
        gate_up(xown, c * HALF + places[i] * KB, half, i == 0)

    def sib_block(i, half):
        cross[i, half].wait_recv()
        gate_up(xsib.at[i], sib * HALF + sib_places[i] * KB, half, False)

    def activate(half):
        for g in range(4):
            k, pc = g % 2, g // 2
            place = pl.ds(half * 256 + g * CAP, CAP)
            gate, up = acc_g[place, :], acc_u[place, :]
            scale = wslot[2 * ((y + 2 * k + half) % NX) + pc][:, 0:1]
            hid[place, :] = (jax.nn.silu(gate) * up * scale).astype(BF16)

    own_block(0, 1)
    for h in range(CHUNKS):
        for step in (1, -1):
            relay_y[h, step].wait_recv()
        forward(h, 2)
    own_block(0, 0)
    for h in range(CHUNKS):
        for dy in (3, 1):
            pass_on(h, dy)
    pass_on(0, 2)
    own_block(1, 1)
    pass_on(1, 2)
    own_block(2, 1)
    pass_on(2, 2)
    sib_block(0, 1)
    pass_on(3, 2)
    sib_block(0, 0)
    own_block(1, 0)
    own_block(2, 0)
    sib_block(1, 1)
    sib_block(2, 1)
    for copy in ring_relay.values():
        copy.wait_recv()
    own_block(3, 0)
    sib_block(1, 0)
    sib_block(2, 0)
    for copy in wide.values():
        copy.wait_recv()
    own_block(3, 1)
    sib_block(3, 0)
    activate(0)
    sib_block(3, 1)
    activate(1)

    pltpu.make_async_copy(wd, wd, local_sem.at[2]).wait()
    ts = (t0, t1, t2)
    at = ((x, y, z), (y, z, x), (z, x, y))
    steps = (
        (lambda d: dev(x + d + NX, y, z, c)),
        (lambda d: dev(x, y + d + NX, z, c)),
        (lambda d: dev(x, y, z + d + NX, c)),
    )
    swap = {}

    def down(n, j, a):
        columns = pl.ds(pl.multiple_of(a * COLS, COLS), COLS)
        w = wd[j, :, columns]
        def rows_of(core):
            first, second = (pl.ds(pl.multiple_of(half * 256 + core * 128, 128), 128) for half in range(2))
            rows = jnp.concatenate([hid[first, :], hid[second, :]], axis=0)
            return jnp.dot(rows, w, preferred_element_type=F32).astype(BF16).reshape(4, CAP, COLS)

        psend[n] = rows_of(sib)
        swap[n] = go(remote(psend.at[n], pcat.at[n, :, pl.ds(CAP, CAP), :], dev(x, y, z, sib)))
        pcat[n, :, 0:CAP, :] = rows_of(c)

    def combine(n, j, a):
        swap[n].wait_recv()
        for i in range(4):
            py = (y + STEPS[i // 2][i % 2]) % NX
            rows = jnp.dot(back[c, py], pcat[n, i], preferred_element_type=F32).astype(BF16)
            for b in range(4):
                part = rows[:, b * 128 : (b + 1) * 128]
                if j == 0:
                    t0[a, py, b] = part
                elif j == 1:
                    t1[py, a, b] = part
                else:
                    t2[a, b, py] = part

    copies = {}
    kinds = ("R1a", "L1a", "R1b", "L1b", "R2", "L2")
    low, high = pl.ds(0, 2), pl.ds(2, 2)
    SPLIT = (pl.ds(0, 64), pl.ds(64, 64))

    def start(j, kind, rows=pl.ds(0, 128), s=0):
        t, place, axis = ts[j], at[j][0], axes[j][0]
        d, half = {
            "R1a": (2, low), "L1a": (2, high), "R1b": (1, high), "L1b": (3, low), "R2": (1, low), "L2": (3, high),
        }[kind]
        copies[j, kind, s] = go(
            remote(
                t.at[(place + d) % NX, half, :, rows],
                rb1.at[j, kinds.index(kind), :, :, rows],
                steps[axis](1 if kind[0] == "R" else -1),
            )
        )

    def middle(j, kind):
        t, place = ts[j], at[j][0]
        copies[j, kind, 0].wait_recv()
        d, half, slot_of, on = (1, low, 0, "R2") if kind == "R1a" else (3, high, 1, "L2")
        for s, rows in enumerate(SPLIT):
            index = (place + d) % NX
            total = t[index, half, :, rows].astype(F32) + rb1[j, slot_of, :, :, rows].astype(F32)
            t[index, half, :, rows] = total.astype(BF16)
            start(j, on, rows, s)

    axes = ((0, 1, 2), (1, 2, 0), (2, 0, 1))

    def args(j, level):
        t = ts[j]
        for l in range(level):
            t = t.at[at[j][l]]
        return (j, level, t, (rb1, rb2, rb3)[level], at[j][level], axes[j][level])

    chunks = [(1, 0, 0), (1, 0, 1), (0, x, 2), (2, z, 2), (1, 0, 2), (1, 0, 3)]
    chunks += [(0, x, 1), (0, x, 3), (2, z, 1), (2, z, 3), (0, x, 0), (2, z, 0)]

    def after(j, k):
        if j == 1:
            for kind in {1: ("R1a", "L1b"), 3: ("L1a", "R1b")}.get(k, ()):
                start(1, kind)
        elif k == 2:
            start(j, "R1a")
            start(j, "L1a")
        elif k == 1:
            start(j, "R1b")
        elif k == 3:
            start(j, "L1b")

    for n in range(len(chunks) + LAG):
        if n < len(chunks):
            j, base, k = chunks[n]
            down(n, j, (base + k) % NX)
        if n >= LAG:
            j, base, k = chunks[n - LAG]
            combine(n - LAG, j, (base + k) % NX)
            after(j, k)

    straight = {}

    def spread(j, level, d, s):
        _, _, t, buf, place, axis = args(j, level)
        lead = (slice(None),) * (level == 1)
        index = (place + d) % NX
        straight[j, level, d, s] = go(
            remote(t.at[(index, *lead, SPLIT[s])], buf.at[(j, d - 1, *lead, SPLIT[s])], steps[axis](d))
        )

    def gather(j, level, s):
        _, _, t, buf, place, _ = args(j, level)
        lead = (slice(None),) * (level == 1)
        total = t[(place, *lead, SPLIT[s])].astype(F32)
        for d in (1, 2, 3):
            straight[j, level, d, s].wait_recv()
            total = total + buf[(j, d - 1, *lead, SPLIT[s])].astype(F32)
        return total.astype(BF16)

    def finish(j, s):
        if s == 0:
            copies[j, "R1b", 0].wait_recv()
            copies[j, "L1b", 0].wait_recv()
        copies[j, "R2", s].wait_recv()
        copies[j, "L2", s].wait_recv()
        here, second, rows = ts[j].at[at[j][0]], at[j][1], SPLIT[s]
        for d in (2, 1, 3, 0):
            b = (second + d) % NX
            one, two = jnp.where(b < 2, 4, 2), jnp.where(b < 2, 3, 5)
            total = here[b, :, rows].astype(F32)
            total = total + rb1[j, one, b % 2, :, rows].astype(F32) + rb1[j, two, b % 2, :, rows].astype(F32)
            here[b, :, rows] = total.astype(BF16)
            if d:
                spread(j, 1, d, s)

    for j, kind in ((1, "R1a"), (0, "R1a"), (0, "L1a"), (2, "R1a"), (2, "L1a"), (1, "L1a")):
        middle(j, kind)
    for s in range(2):
        for j in (0, 2, 1):
            finish(j, s)
    for s in range(2):
        for j in (0, 2, 1):
            ts[j][at[j][0], at[j][1], :, SPLIT[s]] = gather(j, 1, s)
            for d in (2, 1, 3):
                spread(j, 2, d, s)
    for s in range(2):
        for j in (0, 2, 1):
            out[SPLIT[s], j * 128 : (j + 1) * 128] = gather(j, 2, s)
    for copy in sent:
        copy.wait_send()


MESSAGES = 7 + 4 * CHUNKS + 4 + 2 * CHUNKS + 6 * CHUNKS + 6 * CHUNKS + 8 + 12 + 60


def local(tokens, experts, mix_weight, w_gate, w_up, w_down):
    any_spec = pl.BlockSpec(memory_space=pl.ANY)
    vmem_spec = pl.BlockSpec(memory_space=pltpu.VMEM)
    return pl.pallas_call(
        kernel,
        out_shape=jax.ShapeDtypeStruct((TG, 384), BF16),
        in_specs=[any_spec, vmem_spec, vmem_spec, any_spec, any_spec, any_spec],
        out_specs=vmem_spec,
        scratch_shapes=[
            pltpu.VMEM((6144, FFS), BF16),
            pltpu.VMEM((6144, FFS), BF16),
            pltpu.VMEM((3, FFS, 2048), BF16),
            pltpu.VMEM((4, 4, 2, TG, KB), BF16),
            pltpu.VMEM((8, 8, TG), F32),
            pltpu.VMEM((8, TG, TG), BF16),
            pltpu.VMEM((2, 4, TG, TG), BF16),
            pltpu.VMEM((8, CAP, 128), F32),
            pltpu.VMEM((512, KB), BF16),
            pltpu.VMEM((4, 512, KB), BF16),
            pltpu.VMEM((4, 512, KB), BF16),
            pltpu.VMEM((512, FFS), F32),
            pltpu.VMEM((512, FFS), F32),
            pltpu.VMEM((512, FFS), BF16),
            pltpu.VMEM((12, 4, 2 * CAP, COLS), BF16),
            pltpu.VMEM((12, 4, CAP, COLS), BF16),
            pltpu.VMEM((4, 4, 4, 128, 128), BF16),
            pltpu.VMEM((4, 4, 4, 128, 128), BF16),
            pltpu.VMEM((4, 4, 4, 128, 128), BF16),
            pltpu.VMEM((3, 6, 2, 4, 128, 128), BF16),
            pltpu.VMEM((3, 3, 4, 128, 128), BF16),
            pltpu.VMEM((3, 3, 128, 128), BF16),
            pltpu.SemaphoreType.DMA((7,)),
            pltpu.SemaphoreType.DMA((MESSAGES,)),
            pltpu.SemaphoreType.DMA((MESSAGES,)),
        ],
        compiler_params=pltpu.CompilerParams(
            collective_id=0, has_side_effects=True, vmem_limit_bytes=62 * 2**20
        ),
        name="expert_layer",
    )(tokens, experts.T, mix_weight.T, w_gate, w_up, w_down)


def solution(mesh):
    placed = (
        P("group", None),
        P("group", None),
        P("group", None),
        P("group", None, "shard"),
        P("group", None, "shard"),
        P("group", "shard", None),
    )
    return jax.shard_map(
        local, mesh=mesh, in_specs=placed, out_specs=P("group", "shard"), check_vma=False
    )
```

```python
import functools

import jax
import jax.numpy as jnp
from jax import lax
from jax.experimental import pallas as pl
from jax.experimental.pallas import tpu as pltpu
from jax.sharding import PartitionSpec as P

MESH = pl.DeviceIdType.MESH
F32, BF16 = jnp.float32, jnp.bfloat16
NX = 4
TG = 128
CAP = 64
KB = 768
FFS = 512
HALF = 3072
CHUNKS = 4
LAG = 2
ROWS = TG // CHUNKS
COLS = 512


def kernel(
    tok, ex, mw, wg_hbm, wu_hbm, wd_hbm, out,
    wg, wu, wd, land, meta, pick, back, wslot, xown, xsend, xsib, acc_g, acc_u, hid,
    pcat, psend, t0, t1, t2, rb1, rb2, rb3,
    local_sem, send_sem, recv_sem,
):
    group, shard = lax.axis_index("group"), lax.axis_index("shard")
    x, y, z, c = shard // NX, group // 2, shard % NX, group % 2
    sib = 1 - c

    def dev(x, y, z, c):
        return ((y % NX) * 2 + c, (x % NX) * NX + z % NX)

    def on_ring(d):
        return dev(x + d * (1 - c) + NX, y, z + d * c + NX, c)

    def ring_place(core):
        return x * (1 - core) + z * core

    r = ring_place(c)

    used = [0]

    def remote(src, dst, device):
        i = used[0]
        used[0] += 1
        return pltpu.make_async_remote_copy(
            src_ref=src, dst_ref=dst, send_sem=send_sem.at[i], recv_sem=recv_sem.at[i],
            device_id=device, device_id_type=MESH,
        )

    sent = []

    def go(copy):
        copy.start()
        sent.append(copy)
        return copy

    def drain(upto=None):
        for copy in sent[:upto]:
            copy.wait_send()
        del sent[:upto]

    peers = [((y + dy) % NX, c if dc == 0 else sib) for dy in range(NX) for dc in range(2) if dy or dc]
    partners = [dev(x, py, z, pc) for py, pc in peers]
    partners += [dev(x + 1, y, z, c), dev(x + NX - 1, y, z, c), dev(x, y, z + 1, c), dev(x, y, z + NX - 1, c)]
    barrier = pltpu.get_barrier_semaphore()
    for partner in partners:
        pl.semaphore_signal(barrier, inc=1, device_id=partner, device_id_type=MESH)

    load_g = pltpu.make_async_copy(wg_hbm.at[0], wg, local_sem.at[0])
    load_u = pltpu.make_async_copy(wu_hbm.at[0], wu, local_sem.at[1])
    own_loads = [
        pltpu.make_async_copy(
            tok.at[:, pl.ds(pl.multiple_of(c * HALF + q * KB, KB), KB)], land.at[q, y, c], local_sem.at[3 + q]
        )
        for q in range(NX)
    ]
    for copy in own_loads:
        copy.start()

    meta[group] = jnp.zeros((8, TG), F32)
    meta[group, 0:2] = ex[...].astype(F32)
    meta[group, 2:4] = mw[...]

    pl.semaphore_wait(barrier, len(partners))

    plans = [go(remote(meta.at[group], meta.at[group], dev(x, py, z, pc))) for py, pc in peers]

    def token_block(core, q, h):
        return tok.at[pl.ds(h * ROWS, ROWS), pl.ds(pl.multiple_of(core * HALF + q * KB, KB), KB)]

    direct = {}

    def send_along_y(h, d, copies):
        for step in (1, -1):
            for dc in range(2):
                core = c if dc == 0 else sib
                q = (ring_place(core) + d) % NX
                copies[h, step, dc] = go(
                    remote(
                        token_block(core, q, h),
                        land.at[q, y, c, pl.ds(h * ROWS, ROWS)],
                        dev(x, y + step + NX, z, core),
                    )
                )

    for h in range(CHUNKS):
        send_along_y(h, 0, direct)
    load_g.start()
    load_u.start()
    across = [
        go(
            remote(
                tok.at[:, pl.ds(pl.multiple_of(sib * HALF + q * KB, KB), KB)], land.at[q, y, c], dev(x, y, z, sib)
            )
        )
        for q in range(NX)
    ]

    def load_down(i, carry):
        j, b = i // 16, i % 16
        place = jnp.where(j == 0, b, (b % NX) * NX + b // NX)
        pltpu.make_async_copy(
            wd_hbm.at[0, :, pl.ds(pl.multiple_of(b * 384 + j * 128, 128), 128)],
            wd.at[j, :, pl.ds(pl.multiple_of(place * 128, 128), 128)],
            local_sem.at[2],
        ).start()
        return carry

    lax.fori_loop(0, 48, load_down, 0)

    STEPS = ((0, 2), (1, 3))

    for copy in plans:
        copy.wait_recv()
    own_e = group.astype(F32)
    sib_e = (2 * y + sib).astype(F32)
    before = lax.broadcasted_iota(jnp.int32, (TG, TG), 0) < lax.broadcasted_iota(jnp.int32, (TG, TG), 1)
    before = jnp.where(before, 1.0, 0.0).astype(BF16)
    slot = lax.broadcasted_iota(jnp.int32, (CAP, TG), 0).astype(F32)
    first, second = meta[:, 0, :], meta[:, 1, :]
    first_w, second_w = meta[:, 2, :], meta[:, 3, :]
    plan = []
    for e in (own_e, sib_e):
        named = jnp.where((first == e) | (second == e), 1.0, 0.0)
        rank = jnp.dot(named.astype(BF16), before, preferred_element_type=F32)
        plan.append(jnp.where(named > 0.5, rank, -1.0))
    weight = jnp.where(first == own_e, first_w, 0.0) + jnp.where(second == own_e, second_w, 0.0)
    for py in range(NX):
        for pc in range(2):
            g = 2 * py + pc
            rows = [jnp.where(p[g : g + 1, :] == slot, 1.0, 0.0) for p in plan]
            onehot = jnp.concatenate(rows, axis=0)
            pick[g] = onehot.astype(BF16)
            back[pc, py] = onehot.T.astype(BF16)
            total = jnp.sum(rows[0] * weight[g : g + 1, :], axis=1, keepdims=True)
            wslot[g] = jnp.broadcast_to(total, (CAP, 128))

    ring_own, relay_y, ring_relay, wide = {}, {}, {}, {}

    def forward(h, dy):
        block = land.at[r, (y + dy) % NX, :, pl.ds(h * ROWS, ROWS)]
        for d in (1, -1):
            ring_own[h, dy, d] = go(remote(block, block, on_ring(d)))

    def pass_on(h, dy):
        for d in (1, -1):
            ring_own[h, dy, d].wait_recv()
            if dy == 2:
                block = land.at[(r - d + NX) % NX, (y + dy) % NX, 1 if d == 1 else 0, pl.ds(h * ROWS, ROWS)]
                ring_relay[h, dy, d] = go(remote(block, block, on_ring(d)))

    for h in range(CHUNKS):
        for dy, step in ((3, 1), (1, -1)):
            for dc in range(2):
                direct[h, step, dc].wait_recv()
            block = land.at[r, (y + dy) % NX, 1 if step == 1 else 0, pl.ds(h * ROWS, ROWS)]
            relay_y[h, step] = go(remote(block, block, dev(x, y + step + NX, z, c)))
            forward(h, dy)
    for h in range(CHUNKS):
        send_along_y(h, 2, wide)
    for copy in own_loads:
        copy.wait()
    for copy in across:
        copy.wait_recv()
    load_g.wait()
    load_u.wait()

    cross = {}

    def select(i, q, half):
        for g in range(4):
            k, pc = g % 2, g // 2
            py = (y + 2 * k + half) % NX
            rows = jnp.dot(pick[2 * py + pc], land[q, py, pc], preferred_element_type=F32).astype(BF16)
            place = pl.ds(half * 256 + g * CAP, CAP)
            xown[place, :] = rows[0:CAP]
            xsend[i, place, :] = rows[CAP:]

        part = pl.ds(half * 256, 256)
        cross[i, half] = go(remote(xsend.at[i, part], xsib.at[i, part], dev(x, y, z, sib)))

    def gate_up(rows_ref, start, half, fresh):
        depth = pl.ds(pl.multiple_of(start, KB), KB)
        place = pl.ds(half * 256, 256)
        rows = rows_ref[place, :]
        for acc, w in ((acc_g, wg), (acc_u, wu)):
            part = jnp.dot(rows, w[depth, :], preferred_element_type=F32)
            if fresh:
                acc[place, :] = part
            else:
                acc[place, :] += part

    order = (0, 1, 3, 2)
    places = [(r + d) % NX for d in order]
    sib_places = [(ring_place(sib) + d) % NX for d in order]

    def own_block(i, half):
        select(i, places[i], half)
        gate_up(xown, c * HALF + places[i] * KB, half, i == 0)

    def sib_block(i, half):
        cross[i, half].wait_recv()
        gate_up(xsib.at[i], sib * HALF + sib_places[i] * KB, half, False)

    def activate(half):
        for g in range(4):
            k, pc = g % 2, g // 2
            place = pl.ds(half * 256 + g * CAP, CAP)
            gate, up = acc_g[place, :], acc_u[place, :]
            scale = wslot[2 * ((y + 2 * k + half) % NX) + pc][:, 0:1]
            hid[pl.ds(pc * 256 + half * 128 + k * CAP, CAP), :] = (jax.nn.silu(gate) * up * scale).astype(BF16)

    own_block(0, 1)
    for h in range(CHUNKS):
        for step in (1, -1):
            relay_y[h, step].wait_recv()
        forward(h, 2)
    own_block(0, 0)
    for h in range(CHUNKS):
        for dy in (3, 1):
            pass_on(h, dy)
    pass_on(0, 2)
    own_block(1, 1)
    pass_on(1, 2)
    own_block(2, 1)
    pass_on(2, 2)
    sib_block(0, 1)
    pass_on(3, 2)
    sib_block(0, 0)
    own_block(1, 0)
    own_block(2, 0)
    sib_block(1, 1)
    sib_block(2, 1)
    for copy in ring_relay.values():
        copy.wait_recv()
    own_block(3, 0)
    sib_block(1, 0)
    sib_block(2, 0)
    for copy in wide.values():
        copy.wait_recv()
    own_block(3, 1)
    sib_block(3, 0)
    activate(0)
    sib_block(3, 1)
    activate(1)

    dispatched = len(sent)

    pltpu.make_async_copy(wd, wd, local_sem.at[2]).wait()
    ts = (t0, t1, t2)
    at = ((x, y, z), (y, z, x), (z, x, y))
    steps = (
        (lambda d: dev(x + d + NX, y, z, c)),
        (lambda d: dev(x, y + d + NX, z, c)),
        (lambda d: dev(x, y, z + d + NX, c)),
    )
    swap = {}

    def down(n, j, a):
        columns = pl.ds(pl.multiple_of(a * COLS, COLS), COLS)
        w = wd[j, :, columns]
        def rows_of(core):
            rows = hid[pl.ds(pl.multiple_of(core * 256, 256), 256), :]
            return jnp.dot(rows, w, preferred_element_type=F32).astype(BF16).reshape(4, CAP, COLS)

        psend[n] = rows_of(sib)
        swap[n] = go(remote(psend.at[n], pcat.at[n, :, pl.ds(CAP, CAP), :], dev(x, y, z, sib)))
        pcat[n, :, 0:CAP, :] = rows_of(c)

    def combine(n, j, a):
        swap[n].wait_recv()
        for i in range(4):
            py = (y + STEPS[i // 2][i % 2]) % NX
            rows = jnp.dot(back[c, py], pcat[n, i], preferred_element_type=F32).astype(BF16)
            for b in range(4):
                part = rows[:, b * 128 : (b + 1) * 128]
                if j == 0:
                    t0[a, py, b] = part
                elif j == 1:
                    t1[py, a, b] = part
                else:
                    t2[a, b, py] = part

    copies = {}
    kinds = ("R1a", "L1a", "R1b", "L1b", "R2", "L2")
    low, high = pl.ds(0, 2), pl.ds(2, 2)
    SPLIT = (pl.ds(0, 64), pl.ds(64, 64))

    def start(j, kind, rows=pl.ds(0, 128), s=0):
        t, place, axis = ts[j], at[j][0], axes[j][0]
        d, half = {
            "R1a": (2, low), "L1a": (2, high), "R1b": (1, high), "L1b": (3, low), "R2": (1, low), "L2": (3, high),
        }[kind]
        copies[j, kind, s] = go(
            remote(
                t.at[(place + d) % NX, half, :, rows],
                rb1.at[j, kinds.index(kind), :, :, rows],
                steps[axis](1 if kind[0] == "R" else -1),
            )
        )

    def middle(j, kind):
        t, place = ts[j], at[j][0]
        copies[j, kind, 0].wait_recv()
        d, half, slot_of, on = (1, low, 0, "R2") if kind == "R1a" else (3, high, 1, "L2")
        for s, rows in enumerate(SPLIT):
            index = (place + d) % NX
            total = t[index, half, :, rows].astype(F32) + rb1[j, slot_of, :, :, rows].astype(F32)
            t[index, half, :, rows] = total.astype(BF16)
            start(j, on, rows, s)

    axes = ((0, 1, 2), (1, 2, 0), (2, 0, 1))

    def args(j, level):
        t = ts[j]
        for l in range(level):
            t = t.at[at[j][l]]
        return (j, level, t, (rb1, rb2, rb3)[level], at[j][level], axes[j][level])

    chunks = [(1, 0, 0), (1, 0, 1), (0, x, 2), (2, z, 2), (1, 0, 2), (1, 0, 3)]
    chunks += [(0, x, 1), (0, x, 3), (2, z, 1), (2, z, 3), (0, x, 0), (2, z, 0)]

    def after(j, k):
        if j == 1:
            for kind in {1: ("R1a", "L1b"), 3: ("L1a", "R1b")}.get(k, ()):
                start(1, kind)
        elif k == 2:
            start(j, "R1a")
            start(j, "L1a")
        elif k == 1:
            start(j, "R1b")
        elif k == 3:
            start(j, "L1b")

    for n in range(len(chunks) + LAG):
        if n < len(chunks):
            j, base, k = chunks[n]
            down(n, j, (base + k) % NX)
        if n >= LAG:
            j, base, k = chunks[n - LAG]
            combine(n - LAG, j, (base + k) % NX)
            after(j, k)

    straight = {}

    def spread(j, level, d, s):
        _, _, t, buf, place, axis = args(j, level)
        lead = (slice(None),) * (level == 1)
        index = (place + d) % NX
        straight[j, level, d, s] = go(
            remote(t.at[(index, *lead, SPLIT[s])], buf.at[(j, d - 1, *lead, SPLIT[s])], steps[axis](d))
        )

    def gather(j, level, s):
        _, _, t, buf, place, _ = args(j, level)
        lead = (slice(None),) * (level == 1)
        total = t[(place, *lead, SPLIT[s])].astype(F32)
        for d in (1, 2, 3):
            straight[j, level, d, s].wait_recv()
            total = total + buf[(j, d - 1, *lead, SPLIT[s])].astype(F32)
        return total.astype(BF16)

    def finish(j, s):
        if s == 0:
            copies[j, "R1b", 0].wait_recv()
            copies[j, "L1b", 0].wait_recv()
        copies[j, "R2", s].wait_recv()
        copies[j, "L2", s].wait_recv()
        here, second, rows = ts[j].at[at[j][0]], at[j][1], SPLIT[s]
        for d in (2, 1, 3, 0):
            b = (second + d) % NX
            one, two = jnp.where(b < 2, 4, 2), jnp.where(b < 2, 3, 5)
            total = here[b, :, rows].astype(F32)
            total = total + rb1[j, one, b % 2, :, rows].astype(F32) + rb1[j, two, b % 2, :, rows].astype(F32)
            here[b, :, rows] = total.astype(BF16)
            if d:
                spread(j, 1, d, s)

    drain(dispatched)
    first_hops = len(sent)
    for j, kind in ((1, "R1a"), (0, "R1a"), (0, "L1a"), (2, "R1a"), (2, "L1a"), (1, "L1a")):
        middle(j, kind)
    drain(first_hops)
    second_hops = len(sent)
    for s in range(2):
        for j in (0, 2, 1):
            finish(j, s)
    drain(second_hops)
    for s in range(2):
        for j in (0, 2, 1):
            ts[j][at[j][0], at[j][1], :, SPLIT[s]] = gather(j, 1, s)
            for d in (2, 1, 3):
                spread(j, 2, d, s)
    drain()
    for s in range(2):
        for j in (0, 2, 1):
            out[SPLIT[s], j * 128 : (j + 1) * 128] = gather(j, 2, s)


MESSAGES = 7 + 4 * CHUNKS + 4 + 2 * CHUNKS + 6 * CHUNKS + 6 * CHUNKS + 8 + 12 + 60


def local(tokens, experts, mix_weight, w_gate, w_up, w_down):
    any_spec = pl.BlockSpec(memory_space=pl.ANY)
    vmem_spec = pl.BlockSpec(memory_space=pltpu.VMEM)
    return pl.pallas_call(
        kernel,
        out_shape=jax.ShapeDtypeStruct((TG, 384), BF16),
        in_specs=[any_spec, vmem_spec, vmem_spec, any_spec, any_spec, any_spec],
        out_specs=vmem_spec,
        scratch_shapes=[
            pltpu.VMEM((6144, FFS), BF16),
            pltpu.VMEM((6144, FFS), BF16),
            pltpu.VMEM((3, FFS, 2048), BF16),
            pltpu.VMEM((4, 4, 2, TG, KB), BF16),
            pltpu.VMEM((8, 8, TG), F32),
            pltpu.VMEM((8, TG, TG), BF16),
            pltpu.VMEM((2, 4, TG, TG), BF16),
            pltpu.VMEM((8, CAP, 128), F32),
            pltpu.VMEM((512, KB), BF16),
            pltpu.VMEM((4, 512, KB), BF16),
            pltpu.VMEM((4, 512, KB), BF16),
            pltpu.VMEM((512, FFS), F32),
            pltpu.VMEM((512, FFS), F32),
            pltpu.VMEM((512, FFS), BF16),
            pltpu.VMEM((12, 4, 2 * CAP, COLS), BF16),
            pltpu.VMEM((12, 4, CAP, COLS), BF16),
            pltpu.VMEM((4, 4, 4, 128, 128), BF16),
            pltpu.VMEM((4, 4, 4, 128, 128), BF16),
            pltpu.VMEM((4, 4, 4, 128, 128), BF16),
            pltpu.VMEM((3, 6, 2, 4, 128, 128), BF16),
            pltpu.VMEM((3, 3, 4, 128, 128), BF16),
            pltpu.VMEM((3, 3, 128, 128), BF16),
            pltpu.SemaphoreType.DMA((7,)),
            pltpu.SemaphoreType.DMA((MESSAGES,)),
            pltpu.SemaphoreType.DMA((MESSAGES,)),
        ],
        compiler_params=pltpu.CompilerParams(
            collective_id=0, has_side_effects=True, vmem_limit_bytes=62 * 2**20
        ),
        name="expert_layer",
    )(tokens, experts.T, mix_weight.T, w_gate, w_up, w_down)


def solution(mesh):
    placed = (
        P("group", None),
        P("group", None),
        P("group", None),
        P("group", None, "shard"),
        P("group", None, "shard"),
        P("group", "shard", None),
    )
    return jax.shard_map(
        local, mesh=mesh, in_specs=placed, out_specs=P("group", "shard"), check_vma=False
    )
```
